32 devices in a mesh: blk: 2 (over x), wide: 4 (over z), rep: 4 (over y, core).
Axes of the slice: x: 2, y: 2, z: 4, core: 2. Of those that a mesh axis runs over, the one named last changes fastest.
Arguments:
- amplitudes: bfloat16 [8192, 4096], P(('rep', 'wide'), 'blk'), may hold values from -6 to 6
- integrals: bfloat16 [8192, 256], P('rep', 'blk'), may hold values from -0.26367188 to 0.26367188
- occ_energy: float32 [400], replicated, may hold values from -1 to -0.2
- virt_energy: float32 [1600], replicated, may hold values from 0.1 to 1
- virt_irrep: int32 [1600], replicated, may hold values from 0 to 3
- ij_pairs: int32 [4096, 2], P(('blk', 'wide')), may hold values from 0 to 399
- ab_pairs: int32 [256, 2], replicated, may hold values from 0 to 1599
- cd_pairs: int32 [8192, 2], P('rep'), may hold values from 0 to 1599
Outputs:
- new_amplitudes: bfloat16 [256, 4096], P(('rep', 'wide'), 'blk')
The draws below stay inside these ranges and needn't reach their ends.
All inputs are finite; a program needn't handle non-finite values.
Results may differ from the reference program's by a relative error of at most 0.012.
Values may be sent and summed in bfloat16 or wider, within the bound.
A program may use at most 64 MiB of HBM per device.

```python
import jax
import jax.numpy as jnp
from jax import lax

OCC = 400
VIRT = 1600
CDQ = 2048
IJ = 4096
CD = 8192
AB = 256
N_REP = 4


def touch_ends(entries, rng, low, top_value):
    extent = entries.shape
    spot = [jax.random.randint(jax.random.fold_in(rng, axis), (), 0, extent[axis]) for axis in range(len(extent))]
    entries = entries.at[tuple(spot)].set(low)
    longest = extent.index(max(extent))
    spot[longest] = (spot[longest] + 1) % extent[longest]
    return entries.at[tuple(spot)].set(top_value)


def block_levels(key, extent, shards, low, high):
    def one(dim, blocks):
        steps = jax.random.uniform(jax.random.fold_in(jax.random.fold_in(key, 6), dim), (blocks,), jnp.float32, low / len(shards), high / len(shards))
        return jnp.repeat(jnp.exp(steps), extent[dim] // blocks).reshape((-1,) + (1,) * (len(extent) - dim - 1))

    loudness = one(*shards[0])
    for cut in shards[1:]:
        loudness = loudness * one(*cut)
    return loudness


def noise(rng, extent, scale, most, cuts=(), held_as=jnp.bfloat16):
    array = jax.random.normal(rng, extent, jnp.float32) * scale
    if len(cuts) > 0:
        array = block_levels(rng, extent, cuts, -0.22, 0.18) * array
    return jnp.clip(array, min=-most, max=most).astype(held_as)


def setup_inputs(seed: int = 0) -> dict:
    arg_keys = jax.random.split(jax.random.key(seed), 9)
    amplitudes = noise(arg_keys[0], (CD, IJ), 1.0, 6.0, ((0, 16), (1, 2)))
    integrals = noise(arg_keys[1], (CD, AB), (4.0 / CD ** 0.5), 0.26367188, ((0, 4), (1, 2)))
    occ_energy = jnp.clip(jax.random.uniform(arg_keys[2], (OCC,), jnp.float32, -1.0, -0.2), -1.0, -0.2)
    virt_energy = jnp.clip(jax.random.uniform(arg_keys[3], (VIRT,), jnp.float32, 0.1, 1.0), 0.1, 1.0)
    virt_irrep = touch_ends(jax.random.randint(arg_keys[4], (VIRT,), 0, 4), jax.random.fold_in(arg_keys[4], 1), 0, 3).astype(jnp.int32)
    ij_pairs = touch_ends(jax.random.randint(arg_keys[5], (IJ, 2), 0, OCC), jax.random.fold_in(arg_keys[5], 1), 0, OCC - 1).astype(jnp.int32)
    ab_pairs = touch_ends(jax.random.randint(arg_keys[6], (AB, 2), 0, VIRT), jax.random.fold_in(arg_keys[6], 1), 0, VIRT - 1).astype(jnp.int32)
    cd_pairs = touch_ends(jax.random.randint(arg_keys[7], (CD, 2), 0, VIRT), jax.random.fold_in(arg_keys[7], 1), 0, VIRT - 1).astype(jnp.int32)
    return {"amplitudes": amplitudes, "integrals": integrals, "occ_energy": occ_energy, "virt_energy": virt_energy, "virt_irrep": virt_irrep, "ij_pairs": ij_pairs, "ab_pairs": ab_pairs, "cd_pairs": cd_pairs}


def reference(amplitudes, integrals, occ_energy, virt_energy, virt_irrep, ij_pairs, ab_pairs, cd_pairs):
    ab_labels = jnp.bitwise_xor(virt_irrep[ab_pairs[:, 0].astype(jnp.int32)], virt_irrep[ab_pairs[:, 1].astype(jnp.int32)])
    cd_labels = jnp.bitwise_xor(virt_irrep[cd_pairs[:, 0].astype(jnp.int32)], virt_irrep[cd_pairs[:, 1].astype(jnp.int32)])
    masked = jnp.where(cd_labels[:, None] == ab_labels[None, :], integrals, jnp.zeros_like(integrals))
    ladder = jnp.zeros((amplitudes.shape[1], integrals.shape[1]), jnp.float32)
    for rep_part in range(N_REP):
        amp_block = amplitudes[rep_part * CDQ:(rep_part + 1) * CDQ]
        slab_block = masked[rep_part * CDQ:(rep_part + 1) * CDQ]
        quarter_term = lax.dot_general(amp_block, slab_block, (((0,), (0,)), ((), ())), preferred_element_type=jnp.float32)
        rounded = lax.optimization_barrier(quarter_term.astype(jnp.bfloat16))
        ladder = ladder + rounded.astype(jnp.float32)
    pair_occ = occ_energy[ij_pairs[:, 0].astype(jnp.int32)] + occ_energy[ij_pairs[:, 1].astype(jnp.int32)]
    pair_virt = virt_energy[ab_pairs[:, 0].astype(jnp.int32)] + virt_energy[ab_pairs[:, 1].astype(jnp.int32)]
    denominator = pair_occ[:, None] - pair_virt[None, :]
    updated = (ladder / denominator).astype(jnp.bfloat16)
    return updated.T
```

```python
import jax
import jax.numpy as jnp
from jax import lax
from jax.experimental import pallas as pl
from jax.experimental.pallas import tpu as pltpu
from jax.sharding import PartitionSpec as P

MESH = pl.DeviceIdType.MESH
DEPTH = 256


def three_parts(values):
    high = values.astype(jnp.bfloat16).astype(jnp.float32)
    rest = values - high
    middle = rest.astype(jnp.bfloat16).astype(jnp.float32)
    return high, middle, rest - middle


def as_rows(rows, extent):
    row = lax.broadcasted_iota(jnp.int32, (16, extent), 0)
    table = jnp.zeros((16, extent), jnp.float32)
    for place, values in enumerate(rows):
        table = jnp.where(row == place, values, table)
    return table.astype(jnp.bfloat16)


def pair_sums(table_ref, first, second):
    extent = table_ref.shape[1]
    pairs = first.shape[1]
    total = jnp.zeros((16, pairs), jnp.float32)
    for start in range(0, extent, DEPTH):
        size = min(DEPTH, extent - start)
        orbital = lax.broadcasted_iota(jnp.int32, (size, pairs), 0) + start
        count = jnp.where(orbital == first, 1.0, 0.0) + jnp.where(orbital == second, 1.0, 0.0)
        total += jnp.dot(
            table_ref[:, start:start + size],
            count.astype(jnp.bfloat16),
            preferred_element_type=jnp.float32,
        )
    return total


def labels_of(sums):
    low = jnp.where(sums[0:1] == 2.0, 0.0, sums[0:1])
    high = jnp.where(sums[1:2] == 2.0, 0.0, sums[1:2])
    return low + 2.0 * high


def ladder_kernel(
    amp_ref, int_ref, occ_ref, virt_ref, irrep_ref, ij_ref, ab_ref, cd_ref, out_ref,
    amp_v, own_v, peer_v, virt_tab, occ_tab, ab_lab, virt_col, occ_all,
    part, part_in, half, half_in, tile, tile_in,
    load_sem, x_sem, core_sem, y_sem, z_sem, occ_sem,
):
    n_chunk, depth, width = amp_v.shape
    n_wide, rows = tile.shape[1], tile.shape[2]
    cols = own_v.shape[1]
    group = half.shape[2]
    b, w, r = lax.axis_index("blk"), lax.axis_index("wide"), lax.axis_index("rep")
    y, c = r // 2, r % 2
    other_b = 1 - b
    sibling = y * 2 + (1 - c)
    across = (1 - y) * 2 + c
    send_step = (b + y + 1) % 2
    keep_step = 1 - send_step
    wides = [(w + k) % n_wide for k in range(n_wide)]

    my_rows = pl.ds(pl.multiple_of(w * depth, depth), depth)
    own_load = pltpu.make_async_copy(int_ref.at[my_rows, :], own_v, load_sem.at[n_chunk])
    own_load.start()
    amp_loads = []
    for j in range(n_chunk):
        load = pltpu.make_async_copy(
            amp_ref.at[:, pl.ds(j * width, width)], amp_v.at[j], load_sem.at[j]
        )
        load.start()
        amp_loads.append(load)

    barrier = pltpu.get_barrier_semaphore()
    partners = [{"blk": other_b}, {"rep": sibling}, {"rep": across}]
    partners += [{"wide": wides[k]} for k in range(1, n_wide)]
    for partner in partners:
        pl.semaphore_signal(barrier, inc=1, device_id=partner, device_id_type=MESH)
    pl.semaphore_wait(barrier, len(partners))

    def remote(src, dst, sems, place, partner):
        return pltpu.make_async_remote_copy(
            src_ref=src,
            dst_ref=dst,
            send_sem=sems.at[(0,) + place],
            recv_sem=sems.at[(1,) + place],
            device_id=partner,
            device_id_type=MESH,
        )

    x_copy = remote(int_ref.at[my_rows, :], peer_v, x_sem, (0,), {"blk": other_b})
    x_copy.start()

    n_virt, n_occ = virt_ref.shape[0], occ_ref.shape[0]
    irrep = irrep_ref[...].reshape(1, n_virt)
    energies = three_parts(virt_ref[...].reshape(1, n_virt))
    bits = ((irrep & 1).astype(jnp.float32), ((irrep >> 1) & 1).astype(jnp.float32))
    virt_tab[...] = as_rows(bits + energies, n_virt)
    occ_tab[...] = as_rows(three_parts(occ_ref[...].reshape(1, n_occ)), n_occ)

    my_lanes = pl.ds(pl.multiple_of(w * depth, depth), depth)
    cd_sums = pair_sums(virt_tab, cd_ref[0:1, my_lanes], cd_ref[1:2, my_lanes])
    cd_label = jnp.broadcast_to(labels_of(cd_sums), (8, depth)).T[:, 0:1]
    ab_sums = pair_sums(virt_tab, ab_ref[0:1, :], ab_ref[1:2, :])
    ab_label = labels_of(ab_sums)
    for h in range(2):
        ab_lab[h] = jnp.broadcast_to(ab_label[:, h * cols:(h + 1) * cols], (8, cols))
    pair_virt = (ab_sums[2:3] + ab_sums[3:4]) + ab_sums[4:5]
    virt_col[...] = jnp.broadcast_to(pair_virt, (8, 2 * cols)).T

    core_copies, y_copies = {}, {}

    def contribute(step, slab_v, column):
        kept = jnp.where(
            cd_label == ab_lab[column][0:1], slab_v[...].astype(jnp.float32), 0.0
        ).T.astype(jnp.bfloat16)
        for j in range(n_chunk):
            if step == 0:
                amp_loads[j].wait()
            product = jnp.dot(kept, amp_v[j], preferred_element_type=jnp.float32)
            product = product.astype(jnp.bfloat16)
            for core in range(2):
                part[step, core, j] = product[core * group:(core + 1) * group]
            copy = remote(
                part.at[step, 1 - c, j], part_in.at[step, j], core_sem, (step, j), {"rep": sibling}
            )
            copy.start()
            core_copies[step, j] = copy

    def y_copy(j):
        return remote(half.at[send_step, j], half_in.at[j], y_sem, (j,), {"rep": across})

    def fold(step):
        for j in range(n_chunk):
            core_copies[step, j].wait()
            half[step, j] = (
                part[step, c, j].astype(jnp.float32) + part_in[step, j].astype(jnp.float32)
            ).astype(jnp.bfloat16)

            @pl.when(send_step == step)
            def _():
                y_copy(j).start()

    own_load.wait()
    contribute(0, own_v, b)
    fold(0)

    occ_sums = pair_sums(occ_tab, ij_ref[0:1, :], ij_ref[1:2, :])
    pair_occ = (occ_sums[0:1] + occ_sums[1:2]) + occ_sums[2:3]
    occ_all[w] = jnp.broadcast_to(pair_occ, (8, width))
    occ_copies = [
        remote(occ_all.at[w], occ_all.at[w], occ_sem, (k,), {"wide": wides[k]})
        for k in range(1, n_wide)
    ]
    for copy in occ_copies:
        copy.start()

    x_copy.wait()
    contribute(1, peer_v, other_b)
    fold(1)

    z_copies = {}
    for j in range(n_chunk):
        y_copy(j).wait()
        total = half[keep_step, j].astype(jnp.float32) + half_in[j].astype(jnp.float32)
        total = total.astype(jnp.bfloat16)
        for i in range(n_wide):
            tile[j, i] = total[i * rows:(i + 1) * rows]
        for k in range(1, n_wide):
            copy = remote(
                tile.at[j, wides[k]], tile_in.at[j, k], z_sem, (j, k), {"wide": wides[k]}
            )
            copy.start()
            z_copies[j, k] = copy

    for copy in occ_copies:
        copy.wait()
    my_virt = virt_col[pl.ds(pl.multiple_of(r * group + w * rows, rows), rows), :][:, 0:1]
    for j in range(n_chunk):
        ladder = tile[j, w].astype(jnp.float32)
        for k in range(1, n_wide):
            z_copies[j, k].wait()
            ladder += tile_in[j, k].astype(jnp.float32)
        out_ref[:, j * width:(j + 1) * width] = (
            ladder / (occ_all[j][0:1] - my_virt)
        ).astype(jnp.bfloat16)


def in_place(
    amplitudes, integrals, occ_energy, virt_energy, virt_irrep, ij_pairs, ab_pairs, cd_pairs
):
    depth, n_ij = amplitudes.shape
    cols = integrals.shape[1]
    n_ab = ab_pairs.shape[0]
    n_wide, n_rep = lax.axis_size("wide"), lax.axis_size("rep")
    width = ij_pairs.shape[0]
    group = n_ab // n_rep
    rows = group // n_wide
    bf16, f32 = jnp.bfloat16, jnp.float32
    vmem, hbm = pl.BlockSpec(memory_space=pltpu.VMEM), pl.BlockSpec(memory_space=pl.ANY)
    dma = pltpu.SemaphoreType.DMA
    return pl.pallas_call(
        ladder_kernel,
        out_shape=jax.ShapeDtypeStruct((rows, n_ij), bf16),
        in_specs=[hbm, hbm] + [vmem] * 6,
        out_specs=vmem,
        scratch_shapes=[
            pltpu.VMEM((n_wide, depth, width), bf16),
            pltpu.VMEM((depth, cols), bf16),
            pltpu.VMEM((depth, cols), bf16),
            pltpu.VMEM((16, virt_energy.shape[0]), bf16),
            pltpu.VMEM((16, occ_energy.shape[0]), bf16),
            pltpu.VMEM((2, 8, cols), f32),
            pltpu.VMEM((n_ab, 8), f32),
            pltpu.VMEM((n_wide, 8, width), f32),
            pltpu.VMEM((2, 2, n_wide, group, width), bf16),
            pltpu.VMEM((2, n_wide, group, width), bf16),
            pltpu.VMEM((2, n_wide, group, width), bf16),
            pltpu.VMEM((n_wide, group, width), bf16),
            pltpu.VMEM((n_wide, n_wide, rows, width), bf16),
            pltpu.VMEM((n_wide, n_wide, rows, width), bf16),
            dma((n_wide + 1,)),
            dma((2, 1)),
            dma((2, 2, n_wide)),
            dma((2, n_wide)),
            dma((2, n_wide, n_wide)),
            dma((2, n_wide)),
        ],
        compiler_params=pltpu.CompilerParams(
            collective_id=0, has_side_effects=True, vmem_limit_bytes=32 * 1024 * 1024
        ),
        name="ladder",
    )(amplitudes, integrals, occ_energy, virt_energy, virt_irrep, ij_pairs.T, ab_pairs.T, cd_pairs.T)


def fits_in_place(amplitudes, integrals, ij_pairs, ab_pairs):
    n_blk, n_wide, n_rep = (lax.axis_size(axis) for axis in ("blk", "wide", "rep"))
    n_ab, n_ij = ab_pairs.shape[0], amplitudes.shape[1]
    return (
        n_blk == 2
        and n_rep == 4
        and integrals.shape[1] * 2 == n_ab
        and integrals.shape[1] % 128 == 0
        and n_ab % (n_rep * n_wide * 16) == 0
        and ij_pairs.shape[0] * n_wide == n_ij
        and ij_pairs.shape[0] % 128 == 0
        and amplitudes.shape[0] % 128 == 0
        and n_ab * n_ij <= 2**20
        and amplitudes.size <= 2**21
    )


def passed_along(block, axis, distance):
    devices = range(lax.axis_size(axis))
    route = [((i - distance) % len(devices), i) for i in devices]
    return lax.ppermute(block, axis, route)


def lookup(indices, source_table):
    matched = indices[:, None] == lax.broadcasted_iota(jnp.int32, (1, source_table.shape[0]), 1)
    return jnp.sum(
        jnp.where(matched, source_table[None, :], jnp.zeros_like(source_table)[None, :]), axis=1
    )


def gathered(
    amplitudes, integrals, occ_energy, virt_energy, virt_irrep, ij_pairs, ab_pairs, cd_pairs
):
    amp_rows = lax.all_to_all(amplitudes, "wide", split_axis=1, concat_axis=0, tiled=True)
    ab_labels = jnp.bitwise_xor(
        lookup(ab_pairs[:, 0], virt_irrep), lookup(ab_pairs[:, 1], virt_irrep)
    )
    cd_labels = jnp.bitwise_xor(
        lookup(cd_pairs[:, 0], virt_irrep), lookup(cd_pairs[:, 1], virt_irrep)
    )
    tile_cols = integrals.shape[1]
    cycle_size = lax.axis_size("blk")
    my_block = lax.axis_index("blk")
    partial_value = jnp.zeros((amp_rows.shape[1], tile_cols * cycle_size), jnp.float32)
    slab_tile = integrals
    for rounds in range(cycle_size):
        source = (my_block - rounds) % cycle_size
        offset = source * tile_cols
        col_labels = lax.dynamic_slice_in_dim(ab_labels, offset, slab_tile.shape[1])
        masked = jnp.where(
            cd_labels[:, None] == col_labels[None, :], slab_tile, jnp.zeros_like(slab_tile)
        )
        partial_value = lax.dynamic_update_slice_in_dim(
            partial_value,
            lax.dot_general(
                amp_rows, masked, (((0,), (0,)), ((), ())), preferred_element_type=jnp.float32
            ),
            offset,
            1,
        )
        if rounds + 1 < cycle_size:
            slab_tile = passed_along(slab_tile, "blk", 1)
    summed = lax.psum_scatter(
        partial_value.astype(jnp.bfloat16), "rep", scatter_dimension=1, tiled=True
    ).astype(jnp.float32)
    quarter = summed.shape[1]
    col_first = lax.axis_index("rep") * quarter
    ab_local = lax.dynamic_slice_in_dim(ab_pairs, col_first, quarter, 0)
    pair_virt = lookup(ab_local[:, 0], virt_energy) + lookup(ab_local[:, 1], virt_energy)
    pair_occ = lookup(ij_pairs[:, 0], occ_energy) + lookup(ij_pairs[:, 1], occ_energy)
    updated = (summed / (pair_occ[:, None] - pair_virt[None, :])).astype(jnp.bfloat16)
    return lax.all_to_all(updated.T, "wide", split_axis=0, concat_axis=1, tiled=True)


def per_device(
    amplitudes, integrals, occ_energy, virt_energy, virt_irrep, ij_pairs, ab_pairs, cd_pairs
):
    plan = in_place if fits_in_place(amplitudes, integrals, ij_pairs, ab_pairs) else gathered
    return plan(
        amplitudes, integrals, occ_energy, virt_energy, virt_irrep, ij_pairs, ab_pairs, cd_pairs
    )


def solution(mesh):
    in_specs = (
        P(("rep", "wide"), "blk"),
        P("rep", "blk"),
        P(),
        P(),
        P(),
        P(("blk", "wide"), None),
        P(),
        P("rep", None),
    )
    out_specs = P(("rep", "wide"), "blk")
    return jax.shard_map(
        per_device, mesh=mesh, in_specs=in_specs, out_specs=out_specs, check_vma=False
    )
```

```python
import jax
import jax.numpy as jnp
from jax import lax
from jax.experimental import pallas as pl
from jax.experimental.pallas import tpu as pltpu
from jax.sharding import PartitionSpec as P

MESH = pl.DeviceIdType.MESH
DEPTH = 256


def three_parts(values):
    high = values.astype(jnp.bfloat16).astype(jnp.float32)
    rest = values - high
    middle = rest.astype(jnp.bfloat16).astype(jnp.float32)
    return high, middle, rest - middle


def as_rows(rows, extent):
    row = lax.broadcasted_iota(jnp.int32, (16, extent), 0)
    table = jnp.zeros((16, extent), jnp.float32)
    for place, values in enumerate(rows):
        table = jnp.where(row == place, values, table)
    return table.astype(jnp.bfloat16)


def pair_sums(table_ref, first, second):
    extent = table_ref.shape[1]
    pairs = first.shape[1]
    total = jnp.zeros((16, pairs), jnp.float32)
    for start in range(0, extent, DEPTH):
        size = min(DEPTH, extent - start)
        orbital = lax.broadcasted_iota(jnp.int32, (size, pairs), 0) + start
        count = jnp.where(orbital == first, 1.0, 0.0) + jnp.where(orbital == second, 1.0, 0.0)
        total += jnp.dot(
            table_ref[:, start:start + size],
            count.astype(jnp.bfloat16),
            preferred_element_type=jnp.float32,
        )
    return total


def labels_of(sums):
    low = jnp.where(sums[0:1] == 2.0, 0.0, sums[0:1])
    high = jnp.where(sums[1:2] == 2.0, 0.0, sums[1:2])
    return low + 2.0 * high


def ladder_kernel(
    amp_hbm, int_hbm, occ_hbm, virt_hbm, irrep_hbm, ij_hbm, ab_hbm, cd_hbm, out_ref,
    occ_ref, virt_ref, irrep_ref, ij_ref, ab_ref, cd_ref, amp_v, own_v, peer_v, virt_tab, occ_tab, ab_lab, virt_col, occ_all,
    part, part_in, half, half_in, tile, tile_in,
    load_sem, x_sem, core_sem, y_sem, z_sem, occ_sem,
):
    n_chunk, depth, width = amp_v.shape
    n_wide, rows = tile.shape[1], tile.shape[2]
    cols = own_v.shape[1]
    group = half.shape[2]
    b, w, r = lax.axis_index("blk"), lax.axis_index("wide"), lax.axis_index("rep")
    y, c = r // 2, r % 2
    other_b = 1 - b
    sibling = y * 2 + (1 - c)
    across = (1 - y) * 2 + c
    send_step = (b + y + 1) % 2
    keep_step = 1 - send_step
    wides = [(w + k) % n_wide for k in range(n_wide)]

    my_rows = pl.ds(pl.multiple_of(w * depth, depth), depth)
    my_lanes = pl.ds(pl.multiple_of(w * depth, depth), depth)
    small = [
        (virt_hbm, virt_ref), (irrep_hbm, irrep_ref), (cd_hbm.at[:, my_lanes], cd_ref),
        (ab_hbm, ab_ref), (occ_hbm, occ_ref), (ij_hbm, ij_ref),
    ]
    small_loads = [
        pltpu.make_async_copy(src, dst, load_sem.at[n_chunk + 1 + place])
        for place, (src, dst) in enumerate(small)
    ]
    for load in small_loads:
        load.start()
    own_load = pltpu.make_async_copy(int_hbm.at[my_rows, :], own_v, load_sem.at[n_chunk])
    own_load.start()
    amp_loads = []
    for j in range(n_chunk):
        load = pltpu.make_async_copy(
            amp_hbm.at[:, pl.ds(j * width, width)], amp_v.at[j], load_sem.at[j]
        )
        load.start()
        amp_loads.append(load)

    barrier = pltpu.get_barrier_semaphore()
    partners = [{"blk": other_b}, {"rep": sibling}, {"rep": across}]
    partners += [{"wide": wides[k]} for k in range(1, n_wide)]
    for partner in partners:
        pl.semaphore_signal(barrier, inc=1, device_id=partner, device_id_type=MESH)
    pl.semaphore_wait(barrier, len(partners))

    def remote(src, dst, sems, place, partner):
        return pltpu.make_async_remote_copy(
            src_ref=src,
            dst_ref=dst,
            send_sem=sems.at[(0,) + place],
            recv_sem=sems.at[(1,) + place],
            device_id=partner,
            device_id_type=MESH,
        )

    x_copy = remote(int_hbm.at[my_rows, :], peer_v, x_sem, (0,), {"blk": other_b})
    x_copy.start()

    for load in small_loads:
        load.wait()
    n_virt, n_occ = virt_ref.shape[0], occ_ref.shape[0]
    irrep = irrep_ref[...].reshape(1, n_virt)
    energies = three_parts(virt_ref[...].reshape(1, n_virt))
    bits = ((irrep & 1).astype(jnp.float32), ((irrep >> 1) & 1).astype(jnp.float32))
    virt_tab[...] = as_rows(bits + energies, n_virt)
    occ_tab[...] = as_rows(three_parts(occ_ref[...].reshape(1, n_occ)), n_occ)

    cd_sums = pair_sums(virt_tab, cd_ref[0:1, :], cd_ref[1:2, :])
    cd_label = jnp.broadcast_to(labels_of(cd_sums), (8, depth)).T[:, 0:1]
    ab_sums = pair_sums(virt_tab, ab_ref[0:1, :], ab_ref[1:2, :])
    ab_label = labels_of(ab_sums)
    for h in range(2):
        ab_lab[h] = jnp.broadcast_to(ab_label[:, h * cols:(h + 1) * cols], (8, cols))
    pair_virt = (ab_sums[2:3] + ab_sums[3:4]) + ab_sums[4:5]
    virt_col[...] = jnp.broadcast_to(pair_virt, (8, 2 * cols)).T

    core_copies, y_copies = {}, {}

    def contribute(step, slab_v, column):
        kept = jnp.where(
            cd_label == ab_lab[column][0:1], slab_v[...].astype(jnp.float32), 0.0
        ).T.astype(jnp.bfloat16)
        for j in range(n_chunk):
            if step == 0:
                amp_loads[j].wait()
            product = jnp.dot(kept, amp_v[j], preferred_element_type=jnp.float32)
            product = product.astype(jnp.bfloat16)
            for core in range(2):
                part[step, core, j] = product[core * group:(core + 1) * group]
            copy = remote(
                part.at[step, 1 - c, j], part_in.at[step, j], core_sem, (step, j), {"rep": sibling}
            )
            copy.start()
            core_copies[step, j] = copy

    def y_copy(j):
        return remote(half.at[send_step, j], half_in.at[j], y_sem, (j,), {"rep": across})

    def fold(step):
        for j in range(n_chunk):
            core_copies[step, j].wait()
            half[step, j] = (
                part[step, c, j].astype(jnp.float32) + part_in[step, j].astype(jnp.float32)
            ).astype(jnp.bfloat16)

            @pl.when(send_step == step)
            def _():
                y_copy(j).start()

    own_load.wait()
    contribute(0, own_v, b)
    fold(0)

    occ_sums = pair_sums(occ_tab, ij_ref[0:1, :], ij_ref[1:2, :])
    pair_occ = (occ_sums[0:1] + occ_sums[1:2]) + occ_sums[2:3]
    occ_all[w] = jnp.broadcast_to(pair_occ, (8, width))
    occ_copies = [
        remote(occ_all.at[w], occ_all.at[w], occ_sem, (k,), {"wide": wides[k]})
        for k in range(1, n_wide)
    ]
    for copy in occ_copies:
        copy.start()

    x_copy.wait()
    contribute(1, peer_v, other_b)
    fold(1)

    z_copies = {}
    for j in range(n_chunk):
        y_copy(j).wait()
        total = half[keep_step, j].astype(jnp.float32) + half_in[j].astype(jnp.float32)
        total = total.astype(jnp.bfloat16)
        for i in range(n_wide):
            tile[j, i] = total[i * rows:(i + 1) * rows]
        for k in range(1, n_wide):
            copy = remote(
                tile.at[j, wides[k]], tile_in.at[j, k], z_sem, (j, k), {"wide": wides[k]}
            )
            copy.start()
            z_copies[j, k] = copy

    for copy in occ_copies:
        copy.wait()
    my_virt = virt_col[pl.ds(pl.multiple_of(r * group + w * rows, rows), rows), :][:, 0:1]
    for j in range(n_chunk):
        ladder = tile[j, w].astype(jnp.float32)
        for k in range(1, n_wide):
            z_copies[j, k].wait()
            ladder += tile_in[j, k].astype(jnp.float32)
        out_ref[:, j * width:(j + 1) * width] = (
            ladder / (occ_all[j][0:1] - my_virt)
        ).astype(jnp.bfloat16)


def in_place(
    amplitudes, integrals, occ_energy, virt_energy, virt_irrep, ij_pairs, ab_pairs, cd_pairs
):
    depth, n_ij = amplitudes.shape
    cols = integrals.shape[1]
    n_ab = ab_pairs.shape[0]
    n_wide, n_rep = lax.axis_size("wide"), lax.axis_size("rep")
    width = ij_pairs.shape[0]
    group = n_ab // n_rep
    rows = group // n_wide
    bf16, f32 = jnp.bfloat16, jnp.float32
    i32 = jnp.int32
    vmem, hbm = pl.BlockSpec(memory_space=pltpu.VMEM), pl.BlockSpec(memory_space=pltpu.HBM)
    dma = pltpu.SemaphoreType.DMA
    return pl.pallas_call(
        ladder_kernel,
        out_shape=jax.ShapeDtypeStruct((rows, n_ij), bf16),
        in_specs=[hbm] * 8,
        out_specs=vmem,
        scratch_shapes=[
            pltpu.VMEM(occ_energy.shape, f32),
            pltpu.VMEM(virt_energy.shape, f32),
            pltpu.VMEM(virt_irrep.shape, i32),
            pltpu.VMEM((2, width), i32),
            pltpu.VMEM((2, n_ab), i32),
            pltpu.VMEM((2, depth), i32),
            pltpu.VMEM((n_wide, depth, width), bf16),
            pltpu.VMEM((depth, cols), bf16),
            pltpu.VMEM((depth, cols), bf16),
            pltpu.VMEM((16, virt_energy.shape[0]), bf16),
            pltpu.VMEM((16, occ_energy.shape[0]), bf16),
            pltpu.VMEM((2, 8, cols), f32),
            pltpu.VMEM((n_ab, 8), f32),
            pltpu.VMEM((n_wide, 8, width), f32),
            pltpu.VMEM((2, 2, n_wide, group, width), bf16),
            pltpu.VMEM((2, n_wide, group, width), bf16),
            pltpu.VMEM((2, n_wide, group, width), bf16),
            pltpu.VMEM((n_wide, group, width), bf16),
            pltpu.VMEM((n_wide, n_wide, rows, width), bf16),
            pltpu.VMEM((n_wide, n_wide, rows, width), bf16),
            dma((n_wide + 7,)),
            dma((2, 1)),
            dma((2, 2, n_wide)),
            dma((2, n_wide)),
            dma((2, n_wide, n_wide)),
            dma((2, n_wide)),
        ],
        compiler_params=pltpu.CompilerParams(
            collective_id=0, has_side_effects=True, vmem_limit_bytes=60 * 1024 * 1024
        ),
        name="ladder",
    )(amplitudes, integrals, occ_energy, virt_energy, virt_irrep, ij_pairs.T, ab_pairs.T, cd_pairs.T)


def fits_in_place(amplitudes, integrals, ij_pairs, ab_pairs):
    n_blk, n_wide, n_rep = (lax.axis_size(axis) for axis in ("blk", "wide", "rep"))
    n_ab, n_ij = ab_pairs.shape[0], amplitudes.shape[1]
    return (
        n_blk == 2
        and n_rep == 4
        and integrals.shape[1] * 2 == n_ab
        and integrals.shape[1] % 128 == 0
        and n_ab % (n_rep * n_wide * 16) == 0
        and ij_pairs.shape[0] * n_wide == n_ij
        and ij_pairs.shape[0] % 128 == 0
        and amplitudes.shape[0] % 128 == 0
        and n_ab * n_ij <= 2**20
        and amplitudes.size <= 2**21
    )


def passed_along(block, axis, distance):
    devices = range(lax.axis_size(axis))
    route = [((i - distance) % len(devices), i) for i in devices]
    return lax.ppermute(block, axis, route)


def lookup(indices, source_table):
    matched = indices[:, None] == lax.broadcasted_iota(jnp.int32, (1, source_table.shape[0]), 1)
    return jnp.sum(
        jnp.where(matched, source_table[None, :], jnp.zeros_like(source_table)[None, :]), axis=1
    )


def gathered(
    amplitudes, integrals, occ_energy, virt_energy, virt_irrep, ij_pairs, ab_pairs, cd_pairs
):
    amp_rows = lax.all_to_all(amplitudes, "wide", split_axis=1, concat_axis=0, tiled=True)
    ab_labels = jnp.bitwise_xor(
        lookup(ab_pairs[:, 0], virt_irrep), lookup(ab_pairs[:, 1], virt_irrep)
    )
    cd_labels = jnp.bitwise_xor(
        lookup(cd_pairs[:, 0], virt_irrep), lookup(cd_pairs[:, 1], virt_irrep)
    )
    tile_cols = integrals.shape[1]
    cycle_size = lax.axis_size("blk")
    my_block = lax.axis_index("blk")
    partial_value = jnp.zeros((amp_rows.shape[1], tile_cols * cycle_size), jnp.float32)
    slab_tile = integrals
    for rounds in range(cycle_size):
        source = (my_block - rounds) % cycle_size
        offset = source * tile_cols
        col_labels = lax.dynamic_slice_in_dim(ab_labels, offset, slab_tile.shape[1])
        masked = jnp.where(
            cd_labels[:, None] == col_labels[None, :], slab_tile, jnp.zeros_like(slab_tile)
        )
        partial_value = lax.dynamic_update_slice_in_dim(
            partial_value,
            lax.dot_general(
                amp_rows, masked, (((0,), (0,)), ((), ())), preferred_element_type=jnp.float32
            ),
            offset,
            1,
        )
        if rounds + 1 < cycle_size:
            slab_tile = passed_along(slab_tile, "blk", 1)
    summed = lax.psum_scatter(
        partial_value.astype(jnp.bfloat16), "rep", scatter_dimension=1, tiled=True
    ).astype(jnp.float32)
    quarter = summed.shape[1]
    col_first = lax.axis_index("rep") * quarter
    ab_local = lax.dynamic_slice_in_dim(ab_pairs, col_first, quarter, 0)
    pair_virt = lookup(ab_local[:, 0], virt_energy) + lookup(ab_local[:, 1], virt_energy)
    pair_occ = lookup(ij_pairs[:, 0], occ_energy) + lookup(ij_pairs[:, 1], occ_energy)
    updated = (summed / (pair_occ[:, None] - pair_virt[None, :])).astype(jnp.bfloat16)
    return lax.all_to_all(updated.T, "wide", split_axis=0, concat_axis=1, tiled=True)


def per_device(
    amplitudes, integrals, occ_energy, virt_energy, virt_irrep, ij_pairs, ab_pairs, cd_pairs
):
    plan = in_place if fits_in_place(amplitudes, integrals, ij_pairs, ab_pairs) else gathered
    return plan(
        amplitudes, integrals, occ_energy, virt_energy, virt_irrep, ij_pairs, ab_pairs, cd_pairs
    )


def solution(mesh):
    in_specs = (
        P(("rep", "wide"), "blk"),
        P("rep", "blk"),
        P(),
        P(),
        P(),
        P(("blk", "wide"), None),
        P(),
        P("rep", None),
    )
    out_specs = P(("rep", "wide"), "blk")
    return jax.shard_map(
        per_device, mesh=mesh, in_specs=in_specs, out_specs=out_specs, check_vma=False
    )
```

```python
import jax
import jax.numpy as jnp
from jax import lax
from jax.experimental import pallas as pl
from jax.experimental.pallas import tpu as pltpu
from jax.sharding import PartitionSpec as P

MESH = pl.DeviceIdType.MESH
DEPTH = 256
LAG = 2
Y_FIRST = ((0, 2), (0, 1, 2))


def three_parts(values):
    high = values.astype(jnp.bfloat16).astype(jnp.float32)
    rest = values - high
    middle = rest.astype(jnp.bfloat16).astype(jnp.float32)
    return high, middle, rest - middle


def as_rows(rows, extent):
    row = lax.broadcasted_iota(jnp.int32, (16, extent), 0)
    table = jnp.zeros((16, extent), jnp.float32)
    for place, values in enumerate(rows):
        table = jnp.where(row == place, values, table)
    return table.astype(jnp.bfloat16)


def pair_sums(table_ref, first, second):
    extent = table_ref.shape[1]
    pairs = first.shape[1]
    total = jnp.zeros((16, pairs), jnp.float32)
    for start in range(0, extent, DEPTH):
        size = min(DEPTH, extent - start)
        orbital = lax.broadcasted_iota(jnp.int32, (size, pairs), 0) + start
        count = jnp.where(orbital == first, 1.0, 0.0) + jnp.where(orbital == second, 1.0, 0.0)
        total += jnp.dot(
            table_ref[:, start:start + size],
            count.astype(jnp.bfloat16),
            preferred_element_type=jnp.float32,
        )
    return total


def labels_of(sums):
    low = jnp.where(sums[0:1] == 2.0, 0.0, sums[0:1])
    high = jnp.where(sums[1:2] == 2.0, 0.0, sums[1:2])
    return low + 2.0 * high


def ladder_kernel(
    amp_hbm, int_hbm, occ_hbm, virt_hbm, irrep_hbm, ij_hbm, ab_hbm, cd_hbm, out_ref,
    occ_ref, virt_ref, irrep_ref, ij_ref, ab_ref, cd_ref, amp_v, own_v, peer_v, virt_tab, occ_tab, ab_lab, virt_col, occ_all,
    part, part_in, half, half_in, tile, tile_in, early, early_in, slim, slim_in,
    load_sem, x_sem, core_sem, y_sem, z_sem, early_sem, slim_sem, occ_sem,
):
    n_chunk, depth, width = amp_v.shape
    n_wide, rows = tile.shape[1], tile.shape[2]
    cols = own_v.shape[1]
    group = half.shape[2]
    b, w, r = lax.axis_index("blk"), lax.axis_index("wide"), lax.axis_index("rep")
    y, c = r // 2, r % 2
    other_b = 1 - b
    sibling = y * 2 + (1 - c)
    across = (1 - y) * 2 + c
    send_step = (b + y + 1) % 2
    wides = [(w + k) % n_wide for k in range(n_wide)]

    my_rows = pl.ds(pl.multiple_of(w * depth, depth), depth)
    my_lanes = pl.ds(pl.multiple_of(w * depth, depth), depth)
    small = [
        (virt_hbm, virt_ref), (irrep_hbm, irrep_ref), (cd_hbm.at[:, my_lanes], cd_ref),
        (ab_hbm, ab_ref), (occ_hbm, occ_ref), (ij_hbm, ij_ref),
    ]
    small_loads = [
        pltpu.make_async_copy(src, dst, load_sem.at[n_chunk + 1 + place])
        for place, (src, dst) in enumerate(small)
    ]
    for load in small_loads:
        load.start()
    own_load = pltpu.make_async_copy(int_hbm.at[my_rows, :], own_v, load_sem.at[n_chunk])
    own_load.start()
    amp_loads = []
    for j in range(n_chunk):
        load = pltpu.make_async_copy(
            amp_hbm.at[:, pl.ds(j * width, width)], amp_v.at[j], load_sem.at[j]
        )
        load.start()
        amp_loads.append(load)

    barrier = pltpu.get_barrier_semaphore()
    partners = [{"blk": other_b}, {"rep": sibling}, {"rep": across}]
    partners += [{"wide": wides[k]} for k in range(1, n_wide)]
    for partner in partners:
        pl.semaphore_signal(barrier, inc=1, device_id=partner, device_id_type=MESH)
    pl.semaphore_wait(barrier, len(partners))

    def remote(src, dst, sems, place, partner):
        return pltpu.make_async_remote_copy(
            src_ref=src,
            dst_ref=dst,
            send_sem=sems.at[(0,) + place],
            recv_sem=sems.at[(1,) + place],
            device_id=partner,
            device_id_type=MESH,
        )

    x_copy = remote(int_hbm.at[my_rows, :], peer_v, x_sem, (0,), {"blk": other_b})
    x_copy.start()

    for load in small_loads:
        load.wait()
    n_virt, n_occ = virt_ref.shape[0], occ_ref.shape[0]
    irrep = irrep_ref[...].reshape(1, n_virt)
    energies = three_parts(virt_ref[...].reshape(1, n_virt))
    bits = ((irrep & 1).astype(jnp.float32), ((irrep >> 1) & 1).astype(jnp.float32))
    virt_tab[...] = as_rows(bits + energies, n_virt)
    occ_tab[...] = as_rows(three_parts(occ_ref[...].reshape(1, n_occ)), n_occ)

    cd_sums = pair_sums(virt_tab, cd_ref[0:1, :], cd_ref[1:2, :])
    cd_label = jnp.broadcast_to(labels_of(cd_sums), (8, depth)).T[:, 0:1]
    ab_sums = pair_sums(virt_tab, ab_ref[0:1, :], ab_ref[1:2, :])
    ab_label = labels_of(ab_sums)
    for h in range(2):
        ab_lab[h] = jnp.broadcast_to(ab_label[:, h * cols:(h + 1) * cols], (8, cols))
    pair_virt = (ab_sums[2:3] + ab_sums[3:4]) + ab_sums[4:5]
    virt_col[...] = jnp.broadcast_to(pair_virt, (8, 2 * cols)).T

    core_copies = {}
    y_first = [[j for j in range(n_chunk) if j % 4 in some] for some in Y_FIRST]
    z_first = [[j for j in range(n_chunk) if j % 4 not in some] for some in Y_FIRST]

    def contribute(step, slab_v, column):
        kept = jnp.where(
            cd_label == ab_lab[column][0:1], slab_v[...].astype(jnp.float32), 0.0
        ).T.astype(jnp.bfloat16)
        for j in range(n_chunk):
            if step == 0:
                amp_loads[j].wait()
            product = jnp.dot(kept, amp_v[j], preferred_element_type=jnp.float32)
            product = product.astype(jnp.bfloat16)
            for core in range(2):
                part[step, core, j] = product[core * group:(core + 1) * group]
            copy = remote(
                part.at[step, 1 - c, j], part_in.at[step, j], core_sem, (step, j), {"rep": sibling}
            )
            copy.start()
            core_copies[step, j] = copy
            if j >= LAG:
                fold(step, j - LAG)
        for j in range(max(n_chunk - LAG, 0), n_chunk):
            fold(step, j)

    def y_copy(j):
        return remote(half.at[send_step, j], half_in.at[j], y_sem, (j,), {"rep": across})

    def slim_copy(j):
        return remote(slim.at[j], slim_in.at[j], slim_sem, (j,), {"rep": across})

    def early_copy(step, j, k):
        return remote(
            early.at[step, j, wides[k]], early_in.at[step, j, k], early_sem, (step, j, k),
            {"wide": wides[k]},
        )

    def fold(step, j):
        core_copies[step, j].wait_recv()
        total = (
            part[step, c, j].astype(jnp.float32) + part_in[step, j].astype(jnp.float32)
        ).astype(jnp.bfloat16)
        if j in y_first[step]:
            half[step, j] = total

            @pl.when(send_step == step)
            def _():
                y_copy(j).start()
        else:
            for i in range(n_wide):
                early[step, j, i] = total[i * rows:(i + 1) * rows]
            for k in range(1, n_wide):
                early_copy(step, j, k).start()

    def wide_sum(step, j):
        ladder = early[step, j, w].astype(jnp.float32)
        for k in range(1, n_wide):
            early_copy(step, j, k).wait_recv()
            ladder += early_in[step, j, k].astype(jnp.float32)
        return ladder

    own_load.wait()
    contribute(0, own_v, b)
    x_copy.wait_recv()
    contribute(1, peer_v, other_b)

    occ_sums = pair_sums(occ_tab, ij_ref[0:1, :], ij_ref[1:2, :])
    pair_occ = (occ_sums[0:1] + occ_sums[1:2]) + occ_sums[2:3]
    occ_all[w] = jnp.broadcast_to(pair_occ, (8, width))
    occ_copies = [
        remote(occ_all.at[w], occ_all.at[w], occ_sem, (k,), {"wide": wides[k]})
        for k in range(1, n_wide)
    ]
    for copy in occ_copies:
        copy.start()

    def z_copy(j, k):
        return remote(
            tile.at[j, wides[k]], tile_in.at[j, k], z_sem, (j, k), {"wide": wides[k]}
        )

    def spread(step):
        for j in y_first[step]:
            y_copy(j).wait_recv()
            total = half[step, j].astype(jnp.float32) + half_in[j].astype(jnp.float32)
            total = total.astype(jnp.bfloat16)
            for i in range(n_wide):
                tile[j, i] = total[i * rows:(i + 1) * rows]
            for k in range(1, n_wide):
                z_copy(j, k).start()

    def cross(step):
        for j in z_first[step]:
            slim[j] = wide_sum(step, j).astype(jnp.bfloat16)
            slim_copy(j).start()

    @pl.when(send_step == 1)
    def _():
        spread(0)
        cross(1)

    @pl.when(send_step == 0)
    def _():
        cross(0)
        spread(1)

    for copy in occ_copies:
        copy.wait_recv()
    my_virt = virt_col[pl.ds(pl.multiple_of(r * group + w * rows, rows), rows), :][:, 0:1]

    def finish(j, ladder):
        out_ref[:, j * width:(j + 1) * width] = (
            ladder / (occ_all[j][0:1] - my_virt)
        ).astype(jnp.bfloat16)

    def gather(step):
        for j in z_first[step]:
            ladder = wide_sum(step, j)
            slim_copy(j).wait_recv()
            finish(j, ladder + slim_in[j].astype(jnp.float32))
        for j in y_first[step]:
            ladder = tile[j, w].astype(jnp.float32)
            for k in range(1, n_wide):
                z_copy(j, k).wait_recv()
                ladder += tile_in[j, k].astype(jnp.float32)
            finish(j, ladder)

    def leave(copies):
        for copy in copies:
            copy.wait_send()

    for step in range(2):
        @pl.when(send_step == 1 - step)
        def _():
            gather(step)
            leave([y_copy(j) for j in y_first[1 - step]])
            leave([slim_copy(j) for j in z_first[1 - step]])
            leave([z_copy(j, k) for j in y_first[step] for k in range(1, n_wide)])

        leave([early_copy(step, j, k) for j in z_first[step] for k in range(1, n_wide)])
    leave([x_copy] + occ_copies + list(core_copies.values()))


def in_place(
    amplitudes, integrals, occ_energy, virt_energy, virt_irrep, ij_pairs, ab_pairs, cd_pairs
):
    depth, n_ij = amplitudes.shape
    cols = integrals.shape[1]
    n_ab = ab_pairs.shape[0]
    n_wide, n_rep = lax.axis_size("wide"), lax.axis_size("rep")
    width = ij_pairs.shape[0]
    group = n_ab // n_rep
    rows = group // n_wide
    bf16, f32 = jnp.bfloat16, jnp.float32
    i32 = jnp.int32
    vmem, hbm = pl.BlockSpec(memory_space=pltpu.VMEM), pl.BlockSpec(memory_space=pltpu.HBM)
    dma = pltpu.SemaphoreType.DMA
    return pl.pallas_call(
        ladder_kernel,
        out_shape=jax.ShapeDtypeStruct((rows, n_ij), bf16),
        in_specs=[hbm] * 8,
        out_specs=vmem,
        scratch_shapes=[
            pltpu.VMEM(occ_energy.shape, f32),
            pltpu.VMEM(virt_energy.shape, f32),
            pltpu.VMEM(virt_irrep.shape, i32),
            pltpu.VMEM((2, width), i32),
            pltpu.VMEM((2, n_ab), i32),
            pltpu.VMEM((2, depth), i32),
            pltpu.VMEM((n_wide, depth, width), bf16),
            pltpu.VMEM((depth, cols), bf16),
            pltpu.VMEM((depth, cols), bf16),
            pltpu.VMEM((16, virt_energy.shape[0]), bf16),
            pltpu.VMEM((16, occ_energy.shape[0]), bf16),
            pltpu.VMEM((2, 8, cols), f32),
            pltpu.VMEM((n_ab, 8), f32),
            pltpu.VMEM((n_wide, 8, width), f32),
            pltpu.VMEM((2, 2, n_wide, group, width), bf16),
            pltpu.VMEM((2, n_wide, group, width), bf16),
            pltpu.VMEM((2, n_wide, group, width), bf16),
            pltpu.VMEM((n_wide, group, width), bf16),
            pltpu.VMEM((n_wide, n_wide, rows, width), bf16),
            pltpu.VMEM((n_wide, n_wide, rows, width), bf16),
            pltpu.VMEM((2, n_wide, n_wide, rows, width), bf16),
            pltpu.VMEM((2, n_wide, n_wide, rows, width), bf16),
            pltpu.VMEM((n_wide, rows, width), bf16),
            pltpu.VMEM((n_wide, rows, width), bf16),
            dma((n_wide + 7,)),
            dma((2, 1)),
            dma((2, 2, n_wide)),
            dma((2, n_wide)),
            dma((2, n_wide, n_wide)),
            dma((2, 2, n_wide, n_wide)),
            dma((2, n_wide)),
            dma((2, n_wide)),
        ],
        compiler_params=pltpu.CompilerParams(
            collective_id=0, has_side_effects=True, vmem_limit_bytes=60 * 1024 * 1024
        ),
        name="ladder",
    )(amplitudes, integrals, occ_energy, virt_energy, virt_irrep, ij_pairs.T, ab_pairs.T, cd_pairs.T)


def fits_in_place(amplitudes, integrals, ij_pairs, ab_pairs):
    n_blk, n_wide, n_rep = (lax.axis_size(axis) for axis in ("blk", "wide", "rep"))
    n_ab, n_ij = ab_pairs.shape[0], amplitudes.shape[1]
    return (
        n_blk == 2
        and n_rep == 4
        and integrals.shape[1] * 2 == n_ab
        and integrals.shape[1] % 128 == 0
        and n_ab % (n_rep * n_wide * 16) == 0
        and ij_pairs.shape[0] * n_wide == n_ij
        and ij_pairs.shape[0] % 128 == 0
        and amplitudes.shape[0] % 128 == 0
        and n_ab * n_ij <= 2**20
        and amplitudes.size <= 2**21
    )


def passed_along(block, axis, distance):
    devices = range(lax.axis_size(axis))
    route = [((i - distance) % len(devices), i) for i in devices]
    return lax.ppermute(block, axis, route)


def lookup(indices, source_table):
    matched = indices[:, None] == lax.broadcasted_iota(jnp.int32, (1, source_table.shape[0]), 1)
    return jnp.sum(
        jnp.where(matched, source_table[None, :], jnp.zeros_like(source_table)[None, :]), axis=1
    )


def gathered(
    amplitudes, integrals, occ_energy, virt_energy, virt_irrep, ij_pairs, ab_pairs, cd_pairs
):
    amp_rows = lax.all_to_all(amplitudes, "wide", split_axis=1, concat_axis=0, tiled=True)
    ab_labels = jnp.bitwise_xor(
        lookup(ab_pairs[:, 0], virt_irrep), lookup(ab_pairs[:, 1], virt_irrep)
    )
    cd_labels = jnp.bitwise_xor(
        lookup(cd_pairs[:, 0], virt_irrep), lookup(cd_pairs[:, 1], virt_irrep)
    )
    tile_cols = integrals.shape[1]
    cycle_size = lax.axis_size("blk")
    my_block = lax.axis_index("blk")
    partial_value = jnp.zeros((amp_rows.shape[1], tile_cols * cycle_size), jnp.float32)
    slab_tile = integrals
    for rounds in range(cycle_size):
        source = (my_block - rounds) % cycle_size
        offset = source * tile_cols
        col_labels = lax.dynamic_slice_in_dim(ab_labels, offset, slab_tile.shape[1])
        masked = jnp.where(
            cd_labels[:, None] == col_labels[None, :], slab_tile, jnp.zeros_like(slab_tile)
        )
        partial_value = lax.dynamic_update_slice_in_dim(
            partial_value,
            lax.dot_general(
                amp_rows, masked, (((0,), (0,)), ((), ())), preferred_element_type=jnp.float32
            ),
            offset,
            1,
        )
        if rounds + 1 < cycle_size:
            slab_tile = passed_along(slab_tile, "blk", 1)
    summed = lax.psum_scatter(
        partial_value.astype(jnp.bfloat16), "rep", scatter_dimension=1, tiled=True
    ).astype(jnp.float32)
    quarter = summed.shape[1]
    col_first = lax.axis_index("rep") * quarter
    ab_local = lax.dynamic_slice_in_dim(ab_pairs, col_first, quarter, 0)
    pair_virt = lookup(ab_local[:, 0], virt_energy) + lookup(ab_local[:, 1], virt_energy)
    pair_occ = lookup(ij_pairs[:, 0], occ_energy) + lookup(ij_pairs[:, 1], occ_energy)
    updated = (summed / (pair_occ[:, None] - pair_virt[None, :])).astype(jnp.bfloat16)
    return lax.all_to_all(updated.T, "wide", split_axis=0, concat_axis=1, tiled=True)


def per_device(
    amplitudes, integrals, occ_energy, virt_energy, virt_irrep, ij_pairs, ab_pairs, cd_pairs
):
    plan = in_place if fits_in_place(amplitudes, integrals, ij_pairs, ab_pairs) else gathered
    return plan(
        amplitudes, integrals, occ_energy, virt_energy, virt_irrep, ij_pairs, ab_pairs, cd_pairs
    )


def solution(mesh):
    in_specs = (
        P(("rep", "wide"), "blk"),
        P("rep", "blk"),
        P(),
        P(),
        P(),
        P(("blk", "wide"), None),
        P(),
        P("rep", None),
    )
    out_specs = P(("rep", "wide"), "blk")
    return jax.shard_map(
        per_device, mesh=mesh, in_specs=in_specs, out_specs=out_specs, check_vma=False
    )
```

```python
import jax
import jax.numpy as jnp
from jax import lax
from jax.experimental import pallas as pl
from jax.experimental.pallas import tpu as pltpu
from jax.sharding import PartitionSpec as P

MESH = pl.DeviceIdType.MESH
DEPTH = 256
LAG = 2
Y_FIRST = ((0, 1), (0, 2, 3))


def three_parts(values):
    high = values.astype(jnp.bfloat16).astype(jnp.float32)
    rest = values - high
    middle = rest.astype(jnp.bfloat16).astype(jnp.float32)
    return high, middle, rest - middle


def as_rows(rows, extent):
    row = lax.broadcasted_iota(jnp.int32, (16, extent), 0)
    table = jnp.zeros((16, extent), jnp.float32)
    for place, values in enumerate(rows):
        table = jnp.where(row == place, values, table)
    return table.astype(jnp.bfloat16)


def pair_sums(table_ref, first, second):
    extent = table_ref.shape[1]
    pairs = first.shape[1]
    total = jnp.zeros((16, pairs), jnp.float32)
    for start in range(0, extent, DEPTH):
        size = min(DEPTH, extent - start)
        orbital = lax.broadcasted_iota(jnp.int32, (size, pairs), 0) + start
        count = jnp.where(orbital == first, 1.0, 0.0) + jnp.where(orbital == second, 1.0, 0.0)
        total += jnp.dot(
            table_ref[:, start:start + size],
            count.astype(jnp.bfloat16),
            preferred_element_type=jnp.float32,
        )
    return total


def labels_of(sums):
    low = jnp.where(sums[0:1] == 2.0, 0.0, sums[0:1])
    high = jnp.where(sums[1:2] == 2.0, 0.0, sums[1:2])
    return low + 2.0 * high


def ladder_kernel(
    amp_hbm, int_hbm, occ_hbm, virt_hbm, irrep_hbm, ij_hbm, ab_hbm, cd_hbm, out_ref,
    occ_ref, virt_ref, irrep_ref, ij_ref, ab_ref, cd_ref, amp_v, own_v, peer_v, virt_tab, occ_tab, ab_lab, virt_col, occ_all,
    part, part_in, half, half_in, tile, tile_in, early, early_in, slim, slim_in,
    load_sem, x_sem, core_sem, y_sem, z_sem, early_sem, slim_sem, occ_sem,
):
    n_chunk, depth, width = amp_v.shape
    n_wide, rows = tile.shape[1], tile.shape[2]
    cols = own_v.shape[1]
    group = half.shape[2]
    b, w, r = lax.axis_index("blk"), lax.axis_index("wide"), lax.axis_index("rep")
    y, c = r // 2, r % 2
    other_b = 1 - b
    sibling = y * 2 + (1 - c)
    across = (1 - y) * 2 + c
    send_step = (b + y + 1) % 2
    wides = [(w + k) % n_wide for k in range(n_wide)]

    my_rows = pl.ds(pl.multiple_of(w * depth, depth), depth)
    my_lanes = pl.ds(pl.multiple_of(w * depth, depth), depth)
    small = [
        (virt_hbm, virt_ref), (irrep_hbm, irrep_ref), (cd_hbm.at[:, my_lanes], cd_ref),
        (ab_hbm, ab_ref), (occ_hbm, occ_ref), (ij_hbm, ij_ref),
    ]
    small_loads = [
        pltpu.make_async_copy(src, dst, load_sem.at[n_chunk + 1 + place])
        for place, (src, dst) in enumerate(small)
    ]
    for load in small_loads:
        load.start()
    own_load = pltpu.make_async_copy(int_hbm.at[my_rows, :], own_v, load_sem.at[n_chunk])
    own_load.start()
    amp_loads = []
    for j in range(n_chunk):
        load = pltpu.make_async_copy(
            amp_hbm.at[:, pl.ds(j * width, width)], amp_v.at[j], load_sem.at[j]
        )
        load.start()
        amp_loads.append(load)

    barrier = pltpu.get_barrier_semaphore()
    partners = [{"blk": other_b}, {"rep": sibling}, {"rep": across}]
    partners += [{"wide": wides[k]} for k in range(1, n_wide)]
    for partner in partners:
        pl.semaphore_signal(barrier, inc=1, device_id=partner, device_id_type=MESH)
    pl.semaphore_wait(barrier, len(partners))

    def remote(src, dst, sems, place, partner):
        return pltpu.make_async_remote_copy(
            src_ref=src,
            dst_ref=dst,
            send_sem=sems.at[(0,) + place],
            recv_sem=sems.at[(1,) + place],
            device_id=partner,
            device_id_type=MESH,
        )

    x_copy = remote(int_hbm.at[my_rows, :], peer_v, x_sem, (0,), {"blk": other_b})
    x_copy.start()

    for load in small_loads:
        load.wait()
    n_virt, n_occ = virt_ref.shape[0], occ_ref.shape[0]
    irrep = irrep_ref[...].reshape(1, n_virt)
    energies = three_parts(virt_ref[...].reshape(1, n_virt))
    bits = ((irrep & 1).astype(jnp.float32), ((irrep >> 1) & 1).astype(jnp.float32))
    virt_tab[...] = as_rows(bits + energies, n_virt)
    occ_tab[...] = as_rows(three_parts(occ_ref[...].reshape(1, n_occ)), n_occ)

    cd_sums = pair_sums(virt_tab, cd_ref[0:1, :], cd_ref[1:2, :])
    cd_label = jnp.broadcast_to(labels_of(cd_sums), (8, depth)).T[:, 0:1]
    ab_sums = pair_sums(virt_tab, ab_ref[0:1, :], ab_ref[1:2, :])
    ab_label = labels_of(ab_sums)
    for h in range(2):
        ab_lab[h] = jnp.broadcast_to(ab_label[:, h * cols:(h + 1) * cols], (8, cols))
    pair_virt = (ab_sums[2:3] + ab_sums[3:4]) + ab_sums[4:5]
    virt_col[...] = jnp.broadcast_to(pair_virt, (8, 2 * cols)).T

    core_copies = {}
    y_first = [[j for j in range(n_chunk) if j % 4 in some] for some in Y_FIRST]
    z_first = [[j for j in range(n_chunk) if j % 4 not in some] for some in Y_FIRST]

    def contribute(step, slab_v, column):
        kept = jnp.where(
            cd_label == ab_lab[column][0:1], slab_v[...].astype(jnp.float32), 0.0
        ).T.astype(jnp.bfloat16)
        for j in range(n_chunk):
            if step == 0:
                amp_loads[j].wait()
            product = jnp.dot(kept, amp_v[j], preferred_element_type=jnp.float32)
            product = product.astype(jnp.bfloat16)
            for core in range(2):
                part[step, core, j] = product[core * group:(core + 1) * group]
            copy = remote(
                part.at[step, 1 - c, j], part_in.at[step, j], core_sem, (step, j), {"rep": sibling}
            )
            copy.start()
            core_copies[step, j] = copy
            if j >= LAG:
                fold(step, j - LAG)
        for j in range(max(n_chunk - LAG, 0), n_chunk):
            fold(step, j)

    def y_copy(j):
        return remote(half.at[send_step, j], half_in.at[j], y_sem, (j,), {"rep": across})

    def slim_copy(j):
        return remote(slim.at[j], slim_in.at[j], slim_sem, (j,), {"rep": across})

    def early_copy(step, j, k):
        return remote(
            early.at[step, j, wides[k]], early_in.at[step, j, k], early_sem, (step, j, k),
            {"wide": wides[k]},
        )

    def fold(step, j):
        core_copies[step, j].wait_recv()
        total = (
            part[step, c, j].astype(jnp.float32) + part_in[step, j].astype(jnp.float32)
        ).astype(jnp.bfloat16)
        if j in y_first[step]:
            half[step, j] = total

            @pl.when(send_step == step)
            def _():
                y_copy(j).start()
        else:
            for i in range(n_wide):
                early[step, j, i] = total[i * rows:(i + 1) * rows]
            for k in range(1, n_wide):
                early_copy(step, j, k).start()

    def wide_sum(step, j):
        ladder = early[step, j, w].astype(jnp.float32)
        for k in range(1, n_wide):
            early_copy(step, j, k).wait_recv()
            ladder += early_in[step, j, k].astype(jnp.float32)
        return ladder

    own_load.wait()
    contribute(0, own_v, b)
    x_copy.wait_recv()
    contribute(1, peer_v, other_b)

    occ_sums = pair_sums(occ_tab, ij_ref[0:1, :], ij_ref[1:2, :])
    pair_occ = (occ_sums[0:1] + occ_sums[1:2]) + occ_sums[2:3]
    occ_all[w] = jnp.broadcast_to(pair_occ, (8, width))
    occ_copies = [
        remote(occ_all.at[w], occ_all.at[w], occ_sem, (k,), {"wide": wides[k]})
        for k in range(1, n_wide)
    ]
    for copy in occ_copies:
        copy.start()

    def z_copy(j, k):
        return remote(
            tile.at[j, wides[k]], tile_in.at[j, k], z_sem, (j, k), {"wide": wides[k]}
        )

    def spread(step):
        for j in y_first[step]:
            y_copy(j).wait_recv()
            total = half[step, j].astype(jnp.float32) + half_in[j].astype(jnp.float32)
            total = total.astype(jnp.bfloat16)
            for i in range(n_wide):
                tile[j, i] = total[i * rows:(i + 1) * rows]
            for k in range(1, n_wide):
                z_copy(j, k).start()

    def cross(step):
        for j in z_first[step]:
            slim[j] = wide_sum(step, j).astype(jnp.bfloat16)
            slim_copy(j).start()

    @pl.when(send_step == 1)
    def _():
        spread(0)
        cross(1)

    @pl.when(send_step == 0)
    def _():
        cross(0)
        spread(1)

    for copy in occ_copies:
        copy.wait_recv()
    my_virt = virt_col[pl.ds(pl.multiple_of(r * group + w * rows, rows), rows), :][:, 0:1]

    def finish(j, ladder):
        out_ref[:, j * width:(j + 1) * width] = (
            ladder / (occ_all[j][0:1] - my_virt)
        ).astype(jnp.bfloat16)

    def gather(step):
        for j in z_first[step]:
            ladder = wide_sum(step, j)
            slim_copy(j).wait_recv()
            finish(j, ladder + slim_in[j].astype(jnp.float32))
        for j in y_first[step]:
            ladder = tile[j, w].astype(jnp.float32)
            for k in range(1, n_wide):
                z_copy(j, k).wait_recv()
                ladder += tile_in[j, k].astype(jnp.float32)
            finish(j, ladder)

    def leave(copies):
        for copy in copies:
            copy.wait_send()

    for step in range(2):
        @pl.when(send_step == 1 - step)
        def _():
            gather(step)
            leave([y_copy(j) for j in y_first[1 - step]])
            leave([slim_copy(j) for j in z_first[1 - step]])
            leave([z_copy(j, k) for j in y_first[step] for k in range(1, n_wide)])

        leave([early_copy(step, j, k) for j in z_first[step] for k in range(1, n_wide)])
    leave([x_copy] + occ_copies + list(core_copies.values()))


def in_place(
    amplitudes, integrals, occ_energy, virt_energy, virt_irrep, ij_pairs, ab_pairs, cd_pairs
):
    depth, n_ij = amplitudes.shape
    cols = integrals.shape[1]
    n_ab = ab_pairs.shape[0]
    n_wide, n_rep = lax.axis_size("wide"), lax.axis_size("rep")
    width = ij_pairs.shape[0]
    group = n_ab // n_rep
    rows = group // n_wide
    bf16, f32 = jnp.bfloat16, jnp.float32
    i32 = jnp.int32
    vmem, hbm = pl.BlockSpec(memory_space=pltpu.VMEM), pl.BlockSpec(memory_space=pltpu.HBM)
    dma = pltpu.SemaphoreType.DMA
    return pl.pallas_call(
        ladder_kernel,
        out_shape=jax.ShapeDtypeStruct((rows, n_ij), bf16),
        in_specs=[hbm] * 8,
        out_specs=vmem,
        scratch_shapes=[
            pltpu.VMEM(occ_energy.shape, f32),
            pltpu.VMEM(virt_energy.shape, f32),
            pltpu.VMEM(virt_irrep.shape, i32),
            pltpu.VMEM((2, width), i32),
            pltpu.VMEM((2, n_ab), i32),
            pltpu.VMEM((2, depth), i32),
            pltpu.VMEM((n_wide, depth, width), bf16),
            pltpu.VMEM((depth, cols), bf16),
            pltpu.VMEM((depth, cols), bf16),
            pltpu.VMEM((16, virt_energy.shape[0]), bf16),
            pltpu.VMEM((16, occ_energy.shape[0]), bf16),
            pltpu.VMEM((2, 8, cols), f32),
            pltpu.VMEM((n_ab, 8), f32),
            pltpu.VMEM((n_wide, 8, width), f32),
            pltpu.VMEM((2, 2, n_wide, group, width), bf16),
            pltpu.VMEM((2, n_wide, group, width), bf16),
            pltpu.VMEM((2, n_wide, group, width), bf16),
            pltpu.VMEM((n_wide, group, width), bf16),
            pltpu.VMEM((n_wide, n_wide, rows, width), bf16),
            pltpu.VMEM((n_wide, n_wide, rows, width), bf16),
            pltpu.VMEM((2, n_wide, n_wide, rows, width), bf16),
            pltpu.VMEM((2, n_wide, n_wide, rows, width), bf16),
            pltpu.VMEM((n_wide, rows, width), bf16),
            pltpu.VMEM((n_wide, rows, width), bf16),
            dma((n_wide + 7,)),
            dma((2, 1)),
            dma((2, 2, n_wide)),
            dma((2, n_wide)),
            dma((2, n_wide, n_wide)),
            dma((2, 2, n_wide, n_wide)),
            dma((2, n_wide)),
            dma((2, n_wide)),
        ],
        compiler_params=pltpu.CompilerParams(
            collective_id=0, has_side_effects=True, vmem_limit_bytes=60 * 1024 * 1024
        ),
        name="ladder",
    )(amplitudes, integrals, occ_energy, virt_energy, virt_irrep, ij_pairs.T, ab_pairs.T, cd_pairs.T)


def fits_in_place(amplitudes, integrals, ij_pairs, ab_pairs):
    n_blk, n_wide, n_rep = (lax.axis_size(axis) for axis in ("blk", "wide", "rep"))
    n_ab, n_ij = ab_pairs.shape[0], amplitudes.shape[1]
    return (
        n_blk == 2
        and n_rep == 4
        and integrals.shape[1] * 2 == n_ab
        and integrals.shape[1] % 128 == 0
        and n_ab % (n_rep * n_wide * 16) == 0
        and ij_pairs.shape[0] * n_wide == n_ij
        and ij_pairs.shape[0] % 128 == 0
        and amplitudes.shape[0] % 128 == 0
        and n_ab * n_ij <= 2**20
        and amplitudes.size <= 2**21
    )


def passed_along(block, axis, distance):
    devices = range(lax.axis_size(axis))
    route = [((i - distance) % len(devices), i) for i in devices]
    return lax.ppermute(block, axis, route)


def lookup(indices, source_table):
    matched = indices[:, None] == lax.broadcasted_iota(jnp.int32, (1, source_table.shape[0]), 1)
    return jnp.sum(
        jnp.where(matched, source_table[None, :], jnp.zeros_like(source_table)[None, :]), axis=1
    )


def gathered(
    amplitudes, integrals, occ_energy, virt_energy, virt_irrep, ij_pairs, ab_pairs, cd_pairs
):
    amp_rows = lax.all_to_all(amplitudes, "wide", split_axis=1, concat_axis=0, tiled=True)
    ab_labels = jnp.bitwise_xor(
        lookup(ab_pairs[:, 0], virt_irrep), lookup(ab_pairs[:, 1], virt_irrep)
    )
    cd_labels = jnp.bitwise_xor(
        lookup(cd_pairs[:, 0], virt_irrep), lookup(cd_pairs[:, 1], virt_irrep)
    )
    tile_cols = integrals.shape[1]
    cycle_size = lax.axis_size("blk")
    my_block = lax.axis_index("blk")
    partial_value = jnp.zeros((amp_rows.shape[1], tile_cols * cycle_size), jnp.float32)
    slab_tile = integrals
    for rounds in range(cycle_size):
        source = (my_block - rounds) % cycle_size
        offset = source * tile_cols
        col_labels = lax.dynamic_slice_in_dim(ab_labels, offset, slab_tile.shape[1])
        masked = jnp.where(
            cd_labels[:, None] == col_labels[None, :], slab_tile, jnp.zeros_like(slab_tile)
        )
        partial_value = lax.dynamic_update_slice_in_dim(
            partial_value,
            lax.dot_general(
                amp_rows, masked, (((0,), (0,)), ((), ())), preferred_element_type=jnp.float32
            ),
            offset,
            1,
        )
        if rounds + 1 < cycle_size:
            slab_tile = passed_along(slab_tile, "blk", 1)
    summed = lax.psum_scatter(
        partial_value.astype(jnp.bfloat16), "rep", scatter_dimension=1, tiled=True
    ).astype(jnp.float32)
    quarter = summed.shape[1]
    col_first = lax.axis_index("rep") * quarter
    ab_local = lax.dynamic_slice_in_dim(ab_pairs, col_first, quarter, 0)
    pair_virt = lookup(ab_local[:, 0], virt_energy) + lookup(ab_local[:, 1], virt_energy)
    pair_occ = lookup(ij_pairs[:, 0], occ_energy) + lookup(ij_pairs[:, 1], occ_energy)
    updated = (summed / (pair_occ[:, None] - pair_virt[None, :])).astype(jnp.bfloat16)
    return lax.all_to_all(updated.T, "wide", split_axis=0, concat_axis=1, tiled=True)


def per_device(
    amplitudes, integrals, occ_energy, virt_energy, virt_irrep, ij_pairs, ab_pairs, cd_pairs
):
    plan = in_place if fits_in_place(amplitudes, integrals, ij_pairs, ab_pairs) else gathered
    return plan(
        amplitudes, integrals, occ_energy, virt_energy, virt_irrep, ij_pairs, ab_pairs, cd_pairs
    )


def solution(mesh):
    in_specs = (
        P(("rep", "wide"), "blk"),
        P("rep", "blk"),
        P(),
        P(),
        P(),
        P(("blk", "wide"), None),
        P(),
        P("rep", None),
    )
    out_specs = P(("rep", "wide"), "blk")
    return jax.shard_map(
        per_device, mesh=mesh, in_specs=in_specs, out_specs=out_specs, check_vma=False
    )
```
